32 devices in a mesh: groups: 2 (over y), region: 4 (over x, core), dev: 4 (over z).
Axes of the slice: x: 2, y: 2, z: 4, core: 2. Of those that a mesh axis runs over, the one named last changes fastest.
Arguments:
- inner_blocks: bfloat16 [32, 192, 128, 128], P(('groups', 'region', 'dev')), parts along dimension 0, may hold values from -1 to 4
- inner_pattern: int32 [32, 2, 192], P(('groups', 'region', 'dev')), parts along dimension 0, may hold values from 0 to 63, as said below
- boundary_blocks: bfloat16 [32, 4, 12, 128, 128], P(('groups', 'region', 'dev')), parts along dimension 0, may hold values from -1 to 1
- boundary_pattern: int32 [32, 4, 2, 12], P(('groups', 'region', 'dev')), parts along dimension 0, may hold values from 0 to 63, as said below
- send_list: int32 [32, 4, 12], P(('groups', 'region', 'dev')), parts along dimension 0, may hold values from 0 to 63, as said below
- right_side: float32 [32, 262144], P(None, ('groups', 'region', 'dev')), parts along dimension 1, may hold values from -48 to 48
- initial: float32 [32, 262144], P(None, ('groups', 'region', 'dev')), parts along dimension 1, may hold values from -3 to 3
Outputs:
- solution: float32 [32, 262144], P(None, ('groups', 'region', 'dev')), parts along dimension 1
- residual: float32 [32, 262144], P(None, ('groups', 'region', 'dev')), parts along dimension 1
The draws below stay inside these ranges and needn't reach their ends.
There are 2 independent parts, one for each index of `groups`. The reference program is written for one: setup_inputs(seed, part) draws one part's arguments, and reference() takes and returns one part's arrays. A program takes and returns all parts, laid end to end along the dimension named above; each array names one. Nothing has to cross between parts.
Inputs may be any that keep to these rules, and one draw needn't show every extreme that they name: `inner_pattern`: inner blocks of each device: entries 0 to 63 are the diagonal blocks (row = column), the rest come in pairs of mutually transposed blocks; Q is symmetric positive definite. `boundary_pattern`: within one device and direction the slots form a permutation of 0 to 11, and each boundary block is the transpose of the matching block on the neighbour. `send_list`: entries of one device and direction are distinct.
All inputs are finite; a program needn't handle non-finite values.
Results may differ from the reference program's by a relative error of at most 0.0017.
The reference program's roundings to bfloat16 on the way count: a program that leaves them out, or rounds other values in their place, can miss the bound.
Values may be sent and summed in bfloat16 or wider, within the bound.
A program may use at most 64 MiB of HBM per device.

```python
import jax
import jax.numpy as jnp
from jax import lax

BLK = 128
CHAINS = 32
B_DEV = 64
HALO = 12
ITERS = 2
NODES = 131072
N_REGION = 4
N_DEV = 4


def grid_roll(values, amount, axis):
    shaped = values.reshape((N_REGION, N_DEV) + values.shape[1:])
    return jnp.roll(shaped, amount, axis=axis).reshape(values.shape)


def structure(key):
    shards = N_REGION * N_DEV
    key_send = jax.random.fold_in(key, 11)
    key_match = jax.random.fold_in(key, 12)
    key_offset = jax.random.fold_in(key, 13)
    scores = jax.random.randint(key_send, (shards, 4, B_DEV), 0, 1 << 20) * B_DEV + jnp.arange(B_DEV, dtype=jnp.int32)
    sending = jnp.argsort(scores, axis=-1)[..., :HALO].astype(jnp.int32)
    mscores = jax.random.randint(key_match, (shards, 2, HALO), 0, 1 << 20) * HALO + jnp.arange(HALO, dtype=jnp.int32)
    matching = jnp.argsort(mscores, axis=-1).astype(jnp.int32)
    offset = jax.random.randint(key_offset, (shards,), 1, B_DEV).astype(jnp.int32)
    return (sending, matching, offset)


def draw_send_list(key, part):
    sending, matching, offset = structure(key)
    return sending


def draw_inner_pattern(key, part):
    sending, matching, offset = structure(key)
    shards = N_REGION * N_DEV
    ordinal = jnp.broadcast_to(jnp.arange(B_DEV, dtype=jnp.int32), (shards, B_DEV))
    moved = (ordinal + offset[:, None]) % B_DEV
    rows = jnp.concatenate([ordinal, ordinal, moved], axis=1)
    columns = jnp.concatenate([ordinal, moved, ordinal], axis=1)
    return jnp.stack([rows, columns], axis=1).astype(jnp.int32)


def draw_boundary_pattern(key, part):
    sending, matching, offset = structure(key)
    shards = N_REGION * N_DEV
    ordinal = jnp.broadcast_to(jnp.arange(HALO, dtype=jnp.int32), (shards, HALO))
    left_rows = jnp.take_along_axis(sending[:, 0], grid_roll(matching[:, 0], 1, 1), axis=-1)
    up_rows = jnp.take_along_axis(sending[:, 2], grid_roll(matching[:, 1], 1, 0), axis=-1)
    pairs = [jnp.stack([left_rows, ordinal], axis=1), jnp.stack([sending[:, 1], matching[:, 0]], axis=1), jnp.stack([up_rows, ordinal], axis=1), jnp.stack([sending[:, 3], matching[:, 1]], axis=1)]
    return jnp.stack(pairs, axis=1).astype(jnp.int32)


def draw_inner_blocks(key, part):
    key = jax.random.fold_in(key, 3)
    shards = N_REGION * N_DEV
    spread = 0.1 / jnp.sqrt(jnp.float32(BLK))
    key_entries, key_diagonal = jax.random.split(key)
    entries = jax.random.uniform(key_entries, (shards, 2, B_DEV, BLK, BLK), jnp.float32, -1.0, 1.0) * (spread * 1.7320508)
    diagonal = jax.random.uniform(key_diagonal, (shards, B_DEV, BLK), jnp.float32, 1.0, 2.0)
    symmetric = (entries[:, 0] + jnp.swapaxes(entries[:, 0], -1, -2)) * 0.70710678
    diagonal_mask = jnp.arange(BLK)[:, None] == jnp.arange(BLK)[None, :]
    diagonal_block = jnp.where(diagonal_mask, diagonal[..., None], symmetric)
    paired = entries[:, 1]
    return jnp.concatenate([diagonal_block, paired, jnp.swapaxes(paired, -1, -2)], axis=1).astype(jnp.bfloat16)


def draw_boundary_blocks(key, part):
    key = jax.random.fold_in(key, 4)
    shards = N_REGION * N_DEV
    spread = 0.1 / jnp.sqrt(jnp.float32(BLK))
    entries = jax.random.uniform(key, (shards, 2, HALO, BLK, BLK), jnp.float32, -1.0, 1.0) * (spread * 1.7320508)
    toward_right = entries[:, 0]
    toward_left = jnp.swapaxes(grid_roll(entries[:, 0], 1, 1), -1, -2)
    toward_below = entries[:, 1]
    toward_above = jnp.swapaxes(grid_roll(entries[:, 1], 1, 0), -1, -2)
    return jnp.stack([toward_left, toward_right, toward_above, toward_below], axis=1).astype(jnp.bfloat16)


def draw_right_side(key, part):
    key = jax.random.fold_in(key, 6)
    total = N_REGION * N_DEV * B_DEV * BLK
    key_noise, key_scale = jax.random.split(key)
    node_index = jnp.arange(total, dtype=jnp.float32) / total
    position_ramp = 1.0 + 2.0 * node_index
    chain_scale = 0.3 * 10.0 ** jax.random.uniform(key_scale, (CHAINS, 1), jnp.float32)
    normal_part = jnp.clip(jax.random.normal(key_noise, (CHAINS, total), jnp.float32), -5.0, 5.0)
    return (normal_part * chain_scale * position_ramp).astype(jnp.float32)


def shard_levels(own_key, shape, cuts, low, top_value):
    level, own = 1.0, jax.random.fold_in(own_key, 6)
    for position, blocks in cuts:
        steps = jnp.exp(jax.random.uniform(jax.random.fold_in(own, position), (blocks,), jnp.float32, low / len(cuts), top_value / len(cuts)))
        level = level * jnp.repeat(steps, shape[position] // blocks).reshape([-1 if axis == position else 1 for axis in range(len(shape))])
    return level


def scatter_about(stream_key, extent, deviation, reach, cuts=(), held_as=jnp.bfloat16):
    array = deviation * jax.random.normal(stream_key, extent, jnp.float32)
    if cuts:
        array = array * shard_levels(stream_key, extent, cuts, -0.22, 0.18)
    return jnp.clip(array, -reach, reach).astype(held_as)


def setup_inputs(seed: int = 0, part: int = 0) -> dict:
    key_of = jax.random.split(jax.random.key(seed), 8)
    part_keys = jax.random.split(jax.random.fold_in(key_of[7], part), 8)
    inner_blocks = draw_inner_blocks(jax.random.fold_in(jax.random.fold_in(key_of[7], part), 71), part)
    inner_pattern = draw_inner_pattern(jax.random.fold_in(jax.random.fold_in(key_of[7], part), 71), part)
    boundary_blocks = draw_boundary_blocks(jax.random.fold_in(jax.random.fold_in(key_of[7], part), 71), part)
    boundary_pattern = draw_boundary_pattern(jax.random.fold_in(jax.random.fold_in(key_of[7], part), 71), part)
    send_list = draw_send_list(jax.random.fold_in(jax.random.fold_in(key_of[7], part), 71), part)
    right_side = draw_right_side(jax.random.fold_in(jax.random.fold_in(key_of[7], part), 71), part)
    initial = scatter_about(part_keys[6], (CHAINS, NODES), 0.5, 3.0, ((1, 16),), jnp.float32)
    return {"inner_blocks": inner_blocks, "inner_pattern": inner_pattern, "boundary_blocks": boundary_blocks, "boundary_pattern": boundary_pattern, "send_list": send_list, "right_side": right_side, "initial": initial}


def pick(view, index):
    return view[:, index]


def per_device(pieces):
    own_view, incoming, inner_tile, inner_map, border_tile, border_map = pieces
    picked = own_view[:, inner_map[1]].astype(jnp.float32)
    product = jnp.einsum("cnv,nwv->ncw", picked, inner_tile.astype(jnp.float32), precision=lax.Precision.HIGHEST)
    summed = jax.ops.segment_sum(product, inner_map[0].astype(jnp.int32), num_segments=B_DEV)
    distant = jnp.stack([incoming[heading][:, border_map[heading, 1]] for heading in range(4)])
    far_product = jnp.einsum("ucev,uewv->uecw", distant.astype(jnp.float32), border_tile.astype(jnp.float32), precision=lax.Precision.HIGHEST)
    summed = summed + jax.ops.segment_sum(far_product.reshape(4 * HALO, CHAINS, BLK), border_map[:, 0].reshape(4 * HALO).astype(jnp.int32), num_segments=B_DEV)
    return summed


def apply_precision(vector, inner_blocks, inner_pattern, boundary_blocks, boundary_pattern, send_list):
    shards = N_REGION * N_DEV
    views = vector.reshape(CHAINS, shards, B_DEV, BLK).transpose(1, 0, 2, 3)
    packets = jax.vmap(pick)(views, send_list)
    arranged = packets.reshape(N_REGION, N_DEV, CHAINS, 4, HALO, BLK)
    from_left = jnp.roll(arranged[:, :, :, 1], 1, axis=1)
    from_right = jnp.roll(arranged[:, :, :, 0], -1, axis=1)
    from_above = jnp.roll(arranged[:, :, :, 3], 1, axis=0)
    from_below = jnp.roll(arranged[:, :, :, 2], -1, axis=0)
    incoming = jnp.stack([from_left, from_right, from_above, from_below], axis=2).reshape(shards, 4, CHAINS, HALO, BLK)
    summed = lax.map(per_device, (views, incoming, inner_blocks, inner_pattern, boundary_blocks, boundary_pattern))
    return summed.transpose(2, 0, 1, 3).reshape(CHAINS, shards * B_DEV * BLK)


def reference(inner_blocks, inner_pattern, boundary_blocks, boundary_pattern, send_list, right_side, initial):
    def apply_now(vector):
        return apply_precision(vector, inner_blocks, inner_pattern, boundary_blocks, boundary_pattern, send_list)

    residual = right_side - apply_now(initial.astype(jnp.bfloat16))
    solution = initial
    direction = residual
    norm_now = jnp.sum(residual * residual, axis=1)
    for iteration in range(ITERS):
        mapped = apply_now(direction.astype(jnp.bfloat16))
        step_length = norm_now / jnp.sum(direction * mapped, axis=1)
        solution = solution + step_length[:, None] * direction
        residual = residual - step_length[:, None] * mapped
        if iteration + 1 < ITERS:
            norm_next = jnp.sum(residual * residual, axis=1)
            direction = residual + (norm_next / norm_now)[:, None] * direction
            norm_now = norm_next
    return solution, residual
```

```python
import functools

import jax
import jax.numpy as jnp
from jax import lax
from jax.experimental import pallas as pl
from jax.experimental.pallas import tpu as pltpu
from jax.sharding import PartitionSpec as P

MESH = pl.DeviceIdType.MESH
ITERS = 2
F32 = jnp.float32
I32 = jnp.int32


def to_sublanes(values, square):
    return jnp.sum(jnp.where(square, values, 0), axis=1, keepdims=True)


def sort_tables(row_lane, col_lane, length):
    lane = lax.broadcasted_iota(I32, (length, length), 1)
    sub = lax.broadcasted_iota(I32, (length, length), 0)
    eye = lane == sub
    key_lane = row_lane * 256 + lax.broadcasted_iota(I32, (1, length), 1)
    key_sub = to_sublanes(key_lane, eye)
    row_sub = to_sublanes(row_lane, eye)
    col_sub = to_sublanes(col_lane, eye)
    rank = jnp.sum(jnp.where(key_lane < key_sub, 1, 0), axis=1, keepdims=True)
    less = jnp.sum(jnp.where(row_lane < row_sub, 1, 0), axis=1, keepdims=True)
    keep = jnp.where(rank == less, 0, 1)
    packed = (key_sub - row_sub * 256) + keep * 256 + col_sub * 512
    order = jnp.sum(jnp.where(rank == lane, packed, 0), axis=0, keepdims=True)
    upto = jnp.sum(jnp.where(row_sub <= lane, 1, 0), axis=0, keepdims=True)
    count = jnp.sum(jnp.where(row_sub == lane, 1, 0), axis=0, keepdims=True)
    return order, upto - 1, count


def kernel(
    nr, nd, inner_hbm, ipat, bnd_hbm, bpat, send_list, rhs_hbm, init_hbm, x_hbm, r_hbm,
    q, qb, x, r, w, d, v, run, runb, prodb, out_box, tab, tab_s, part, slots,
    local_sem, out_sem, in_sem, red_out, red_in, *in_box,
):
    n_inner = q.shape[0]
    halo = out_box.shape[2]
    n_bnd = 4 * halo
    blocks = v.shape[0]
    chains = v.shape[1]
    n_all = nr * nd
    region, dev = lax.axis_index("region"), lax.axis_index("dev")
    me = region * nd + dev

    chunk = n_inner // 4
    loads = [pltpu.make_async_copy(init_hbm, x, local_sem.at[0])]
    for i in range(4):
        part_of = pl.ds(i * chunk, chunk)
        loads.append(pltpu.make_async_copy(inner_hbm.at[0, part_of], q.at[part_of], local_sem.at[1 + i]))
    loads.append(pltpu.make_async_copy(bnd_hbm.at[0], qb, local_sem.at[5]))
    loads.append(pltpu.make_async_copy(rhs_hbm, r, local_sem.at[6]))
    for load in loads:
        load.start()

    def greet(t, _):
        peer = lax.rem(me + t, n_all)
        pl.semaphore_signal(
            barrier, inc=1, device_id={"region": peer // nd, "dev": lax.rem(peer, nd)}, device_id_type=MESH
        )
        return 0

    barrier = pltpu.get_barrier_semaphore()
    lax.fori_loop(1, n_all, greet, 0)

    order, last, count = sort_tables(ipat[0, 1:2, :], ipat[0, 0:1, :], n_inner)
    tab[0:1, 0:n_inner] = order
    tab[1:2, 0:n_inner] = jnp.where(count > 0, last, n_inner)
    lane128 = lax.broadcasted_iota(I32, (1, 128), 1)
    brow = jnp.full((1, 128), 1 << 20, I32)
    for k in range(4):
        for e in range(halo):
            brow = jnp.where(lane128 == k * halo + e, bpat[0, k, 0, e], brow)
    order, last, count = sort_tables(brow, jnp.zeros((1, 128), I32), 128)
    tab[2:3, 0:128] = order
    tab[3:4, 0:128] = jnp.where(count > 0, last, n_bnd)
    tables = pltpu.make_async_copy(tab, tab_s, local_sem.at[7])
    tables.start()
    run[n_inner] = jnp.zeros((chains, 128), F32)
    runb[n_bnd] = jnp.zeros((chains, 128), F32)

    targets = (
        {"dev": lax.rem(dev + nd - 1, nd)},
        {"dev": lax.rem(dev + 1, nd)},
        {"region": lax.rem(region + nr - 1, nr)},
        {"region": lax.rem(region + 1, nr)},
    )
    arrives_at = (1, 0, 3, 2)

    def cols(b):
        return pl.ds(pl.multiple_of(b * 128, 128), 128)

    def box_copy(turn, k):
        return pltpu.make_async_remote_copy(
            src_ref=out_box.at[turn, k],
            dst_ref=in_box[turn * 4 + arrives_at[k]],
            send_sem=out_sem.at[turn, k],
            recv_sem=in_sem.at[turn, arrives_at[k]],
            device_id=targets[k],
            device_id_type=MESH,
        )

    def send_halo(turn):
        for k in (0, 1, 2, 3):
            for e in range(halo):
                out_box[turn, k, e] = v[send_list[0, k, e]]
            box_copy(turn, k).start()

    def apply_parts(turn):
        def inner_step(s, acc):
            word = tab_s[0, s]
            entry, keep, col = word & 255, (word >> 8) & 1, word >> 9
            product = jnp.dot(v[col], q[entry], preferred_element_type=F32)
            acc = jnp.where(jnp.full((chains, 128), keep) != 0, acc, 0.0) + product
            run[s] = acc
            return acc

        lax.fori_loop(0, n_inner, inner_step, jnp.zeros((chains, 128), F32), unroll=8)
        for k in (2, 3, 0, 1):
            box_copy(turn, arrives_at[k]).wait_recv()

            def far_step(e, _):
                prodb[k * halo + e] = lax.dot_general(
                    in_box[turn * 4 + k][bpat[0, k, 1, e]],
                    qb[k, e],
                    (((1,), (1,)), ((), ())),
                    preferred_element_type=F32,
                )
                return 0

            lax.fori_loop(0, halo, far_step, 0, unroll=True)

        def gather_step(s, acc):
            word = tab_s[2, s]
            entry, keep = word & 255, (word >> 8) & 1
            acc = jnp.where(jnp.full((chains, 128), keep) != 0, acc, 0.0) + prodb[entry]
            runb[s] = acc
            return acc

        lax.fori_loop(0, n_bnd, gather_step, jnp.zeros((chains, 128), F32), unroll=8)

    def mapped_of(b):
        return run[tab_s[1, b]] + runb[tab_s[3, b]]

    chain = lax.broadcasted_iota(I32, (chains, 128), 0)
    lane = lax.broadcasted_iota(I32, (chains, 128), 1)

    def all_sum(turn, sums):
        packed = jnp.zeros((chains, 128), F32)
        for j, value in enumerate(sums):
            packed = packed + jnp.where(
                lane == chain + j * chains, jnp.sum(value, axis=1, keepdims=True), 0.0
            )
        row = jnp.sum(packed, axis=0, keepdims=True)
        part[turn] = row
        slots[turn, me] = row

        def copy_to(t):
            peer = lax.rem(me + t, n_all)
            return pltpu.make_async_remote_copy(
                src_ref=part.at[turn],
                dst_ref=slots.at[turn, me],
                send_sem=red_out.at[turn, peer],
                recv_sem=red_in.at[turn, me],
                device_id={"region": peer // nd, "dev": lax.rem(peer, nd)},
                device_id_type=MESH,
            )

        def copy_from(t):
            peer = lax.rem(me + t, n_all)
            return pltpu.make_async_remote_copy(
                src_ref=part.at[turn],
                dst_ref=slots.at[turn, peer],
                send_sem=red_out.at[turn, peer],
                recv_sem=red_in.at[turn, peer],
                device_id={"region": peer // nd, "dev": lax.rem(peer, nd)},
                device_id_type=MESH,
            )

        def start(t, _):
            copy_to(t).start()
            return 0

        def finish(t, _):
            copy_from(t).wait()
            return 0

        lax.fori_loop(1, n_all, start, 0)
        lax.fori_loop(1, n_all, finish, 0)
        total = jnp.sum(slots[turn].reshape(n_all, 128), axis=0, keepdims=True)
        return [
            jnp.sum(jnp.where(lane == chain + j * chains, total, 0.0), axis=1, keepdims=True)
            for j in range(len(sums))
        ]

    zero = jnp.zeros((chains, 128), F32)

    loads[0].wait()

    def round_step(b, _):
        v[b] = x[:, cols(b)].astype(jnp.bfloat16)
        return 0

    lax.fori_loop(0, blocks, round_step, 0, unroll=4)
    pl.semaphore_wait(barrier, n_all - 1)
    send_halo(0)
    tables.wait()
    for load in loads[1:]:
        load.wait()
    apply_parts(0)

    def first_step(b, rr):
        value = r[:, cols(b)] - mapped_of(b)
        r[:, cols(b)] = value
        v[b] = value.astype(jnp.bfloat16)
        return rr + value * value

    rr = lax.fori_loop(0, blocks, first_step, zero, unroll=4)

    send_halo(1)
    apply_parts(1)

    def dots_step(b, sums):
        value = mapped_of(b)
        res = r[:, cols(b)]
        w[:, cols(b)] = value
        return sums[0] + res * value, sums[1] + value * value

    rw, ww = lax.fori_loop(0, blocks, dots_step, (zero, zero), unroll=4)
    norm, cross, square = all_sum(0, (rr, rw, ww))
    step = norm / cross
    norm_next = norm - 2.0 * step * cross + step * step * square
    ratio = norm_next / norm
    step_b = jnp.broadcast_to(step, (chains, 128))
    ratio_b = jnp.broadcast_to(ratio, (chains, 128))

    def update_step(b, rr):
        old = r[:, cols(b)]
        value = old - step_b * w[:, cols(b)]
        along = value + ratio_b * old
        x[:, cols(b)] = x[:, cols(b)] + step_b * old
        r[:, cols(b)] = value
        d[:, cols(b)] = along
        v[b] = along.astype(jnp.bfloat16)
        return rr + value * value

    rr = lax.fori_loop(0, blocks, update_step, zero, unroll=4)

    send_halo(2)
    apply_parts(2)

    def last_dot_step(b, total):
        value = mapped_of(b)
        w[:, cols(b)] = value
        return total + d[:, cols(b)] * value

    dw = lax.fori_loop(0, blocks, last_dot_step, zero, unroll=4)
    norm, curve = all_sum(1, (rr, dw))
    step_c = jnp.broadcast_to(norm / curve, (chains, 128))

    def end_step(b, _):
        x[:, cols(b)] = x[:, cols(b)] + step_c * d[:, cols(b)]
        r[:, cols(b)] = r[:, cols(b)] - step_c * w[:, cols(b)]
        return 0

    lax.fori_loop(0, blocks, end_step, 0, unroll=4)
    stores = [
        pltpu.make_async_copy(x, x_hbm, local_sem.at[8]),
        pltpu.make_async_copy(r, r_hbm, local_sem.at[9]),
    ]
    for store in stores:
        store.start()
    for turn in range(3):
        for k in range(4):
            box_copy(turn, k).wait_send()
    for store in stores:
        store.wait()


def per_device(nr, nd, inner_blocks, inner_pattern, boundary_blocks, boundary_pattern, send_list, right_side, initial):
    n_inner, blk = inner_blocks.shape[1], inner_blocks.shape[2]
    halo = send_list.shape[2]
    chains, nodes = right_side.shape
    blocks = nodes // blk
    n_all = nr * nd
    anywhere = pl.BlockSpec(memory_space=pl.ANY)
    smem = pl.BlockSpec(memory_space=pltpu.SMEM)
    vmem = pl.BlockSpec(memory_space=pltpu.VMEM)
    vector = pltpu.VMEM((chains, nodes), F32)
    return pl.pallas_call(
        functools.partial(kernel, nr, nd),
        out_shape=(
            jax.ShapeDtypeStruct((chains, nodes), F32),
            jax.ShapeDtypeStruct((chains, nodes), F32),
        ),
        in_specs=[anywhere, vmem, anywhere, smem, smem, anywhere, anywhere],
        out_specs=(anywhere, anywhere),
        scratch_shapes=[
            pltpu.VMEM((n_inner, blk, blk), jnp.bfloat16),
            pltpu.VMEM((4, halo, blk, blk), jnp.bfloat16),
            vector,
            vector,
            vector,
            vector,
            pltpu.VMEM((blocks, chains, blk), jnp.bfloat16),
            pltpu.VMEM((n_inner + 1, chains, blk), F32),
            pltpu.VMEM((4 * halo + 1, chains, blk), F32),
            pltpu.VMEM((4 * halo, chains, blk), F32),
            pltpu.VMEM((3, 4, halo, chains, blk), jnp.bfloat16),
            pltpu.VMEM((8, 256), I32),
            pltpu.SMEM((8, 256), I32),
            pltpu.VMEM((ITERS, 1, 128), F32),
            pltpu.VMEM((ITERS, n_all, 1, 128), F32),
            pltpu.SemaphoreType.DMA((10,)),
            pltpu.SemaphoreType.DMA((3, 4)),
            pltpu.SemaphoreType.DMA((3, 4)),
            pltpu.SemaphoreType.DMA((ITERS, n_all)),
            pltpu.SemaphoreType.DMA((ITERS, n_all)),
        ]
        + [pltpu.VMEM((halo, chains, blk), jnp.bfloat16)] * 12,
        compiler_params=pltpu.CompilerParams(
            collective_id=0, has_side_effects=True, vmem_limit_bytes=48 * 1024 * 1024
        ),
    )(inner_blocks, inner_pattern, boundary_blocks, boundary_pattern, send_list, right_side, initial)


def solution(mesh):
    spread = ("groups", "region", "dev")
    return jax.shard_map(
        functools.partial(per_device, mesh.shape["region"], mesh.shape["dev"]),
        mesh=mesh,
        in_specs=(
            P(spread, None, None, None),
            P(spread, None, None),
            P(spread, None, None, None, None),
            P(spread, None, None, None),
            P(spread, None, None),
            P(None, spread),
            P(None, spread),
        ),
        out_specs=(P(None, spread), P(None, spread)),
        check_vma=False,
    )
```

```python
import functools

import jax
import jax.numpy as jnp
from jax import lax
from jax.experimental import pallas as pl
from jax.experimental.pallas import tpu as pltpu
from jax.sharding import PartitionSpec as P

MESH = pl.DeviceIdType.MESH
ITERS = 2
F32 = jnp.float32
I32 = jnp.int32


def to_sublanes(values, square):
    return jnp.sum(jnp.where(square, values, 0), axis=1, keepdims=True)


def sort_tables(row_lane, col_lane, length):
    lane = lax.broadcasted_iota(I32, (length, length), 1)
    sub = lax.broadcasted_iota(I32, (length, length), 0)
    eye = lane == sub
    key_lane = row_lane * 256 + lax.broadcasted_iota(I32, (1, length), 1)
    key_sub = to_sublanes(key_lane, eye)
    row_sub = to_sublanes(row_lane, eye)
    col_sub = to_sublanes(col_lane, eye)
    rank = jnp.sum(jnp.where(key_lane < key_sub, 1, 0), axis=1, keepdims=True)
    less = jnp.sum(jnp.where(row_lane < row_sub, 1, 0), axis=1, keepdims=True)
    keep = jnp.where(rank == less, 0, 1)
    packed = (key_sub - row_sub * 256) + keep * 256 + col_sub * 512
    order = jnp.sum(jnp.where(rank == lane, packed, 0), axis=0, keepdims=True)
    upto = jnp.sum(jnp.where(row_sub <= lane, 1, 0), axis=0, keepdims=True)
    count = jnp.sum(jnp.where(row_sub == lane, 1, 0), axis=0, keepdims=True)
    return order, upto - 1, count


def kernel(
    nr, nd, inner_hbm, ipat_hbm, bnd_hbm, bpat_hbm, send_hbm, rhs_hbm, init_hbm, x_hbm, r_hbm, d_hbm, w_hbm, alpha_hbm,
    ipat, bpat, send_list, q, qb, r, wb, x, rhs, w, d, alpha, v, run, runb, prodb, out_box, tab, tab_s, slots,
    local_sem, out_sem, in_sem, sems, *in_box,
):
    n_inner = q.shape[0]
    halo = out_box.shape[2]
    n_bnd = 4 * halo
    blocks = v.shape[0]
    chains = v.shape[1]
    region, dev = lax.axis_index("region"), lax.axis_index("dev")
    n_all = nr * nd
    me = region * nd + dev

    def each_peer(action):
        if n_all <= 16:
            for t in range(1, n_all):
                action(t)
        else:
            lax.fori_loop(1, n_all, lambda t, _: (action(t), 0)[1], 0)

    chunk = n_inner // 4
    loads = [pltpu.make_async_copy(init_hbm, x, local_sem.at[0])]
    for i in range(4):
        part_of = pl.ds(i * chunk, chunk)
        loads.append(pltpu.make_async_copy(inner_hbm.at[0, part_of], q.at[part_of], local_sem.at[1 + i]))
    loads.append(pltpu.make_async_copy(bnd_hbm.at[0], qb, local_sem.at[5]))
    loads.append(pltpu.make_async_copy(rhs_hbm, rhs, local_sem.at[6]))
    patterns = [
        pltpu.make_async_copy(ipat_hbm, ipat, local_sem.at[10]),
        pltpu.make_async_copy(bpat_hbm, bpat, local_sem.at[11]),
        pltpu.make_async_copy(send_hbm, send_list, local_sem.at[12]),
    ]
    for load in patterns + loads[:1]:
        load.start()

    barrier = pltpu.get_barrier_semaphore()
    def greet(t):
        peer = lax.rem(me + t, n_all)
        pl.semaphore_signal(
            barrier, inc=1, device_id={"region": peer // nd, "dev": lax.rem(peer, nd)}, device_id_type=MESH
        )

    each_peer(greet)

    targets = (
        {"dev": lax.rem(dev + nd - 1, nd)},
        {"dev": lax.rem(dev + 1, nd)},
        {"region": lax.rem(region + nr - 1, nr)},
        {"region": lax.rem(region + 1, nr)},
    )
    arrives_at = (1, 0, 3, 2)

    def cols(b):
        return pl.ds(pl.multiple_of(b * 128, 128), 128)

    def box_copy(turn, k):
        return pltpu.make_async_remote_copy(
            src_ref=out_box.at[turn, k],
            dst_ref=in_box[turn * 4 + arrives_at[k]],
            send_sem=out_sem.at[turn, k],
            recv_sem=in_sem.at[turn, arrives_at[k]],
            device_id=targets[k],
            device_id_type=MESH,
        )

    def send_halo(turn, block_of):
        for k in (0, 1, 2, 3):
            for e in range(halo):
                out_box[turn, k, e] = block_of(send_list[0, k, e]).astype(jnp.bfloat16)
            if turn == 0 and k == 0:
                pl.semaphore_wait(barrier, n_all - 1)
            box_copy(turn, k).start()

    def apply_parts(turn):
        def inner_step(s, acc):
            word = tab_s[0, s]
            entry, keep, col = word & 255, (word >> 8) & 1, word >> 9
            product = jnp.dot(v[col], q[entry], preferred_element_type=F32)
            acc = jnp.where(jnp.full((chains, 128), keep) != 0, acc, 0.0) + product
            run[s] = acc
            return acc

        lax.fori_loop(0, n_inner, inner_step, jnp.zeros((chains, 128), F32), unroll=32)
        for k in (2, 3, 0, 1):
            box_copy(turn, arrives_at[k]).wait_recv()

            def far_step(e, _):
                prodb[k * halo + e] = lax.dot_general(
                    in_box[turn * 4 + k][bpat[0, k, 1, e]],
                    qb[k, e],
                    (((1,), (1,)), ((), ())),
                    preferred_element_type=F32,
                )
                return 0

            lax.fori_loop(0, halo, far_step, 0, unroll=True)

        def gather_step(s, acc):
            word = tab_s[2, s]
            entry, keep = word & 255, (word >> 8) & 1
            acc = jnp.where(jnp.full((chains, 128), keep) != 0, acc, 0.0) + prodb[entry]
            runb[s] = acc
            return acc

        lax.fori_loop(0, n_bnd, gather_step, jnp.zeros((chains, 128), F32), unroll=8)

    def mapped_of(b):
        return run[tab_s[1, b]] + runb[tab_s[3, b]]

    chain = lax.broadcasted_iota(I32, (chains, 128), 0)
    lane = lax.broadcasted_iota(I32, (chains, 128), 1)

    def all_sum(turn, sums):
        packed = jnp.zeros((chains, 128), F32)
        for j, value in enumerate(sums):
            packed = packed + jnp.where(
                lane == chain + j * chains, jnp.sum(value, axis=1, keepdims=True), 0.0
            )
        row = jnp.sum(packed, axis=0, keepdims=True)
        slots[turn, me] = row

        def copy(t, at):
            peer = lax.rem(me + t, n_all)
            slot = me if at else peer
            return pltpu.make_async_remote_copy(
                src_ref=slots.at[turn, me],
                dst_ref=slots.at[turn, slot],
                send_sem=sems.at[turn, 0, peer],
                recv_sem=sems.at[turn, 1, slot],
                device_id={"region": peer // nd, "dev": lax.rem(peer, nd)},
                device_id_type=MESH,
            )

        each_peer(lambda t: copy(t, True).start())
        unsent.append(lambda: each_peer(lambda t: copy(t, True).wait_send()))

        def finish():
            each_peer(lambda t: copy(t, False).wait_recv())
            total = jnp.sum(slots[turn].reshape(n_all, 128), axis=0, keepdims=True)
            return [
                jnp.sum(jnp.where(lane == chain + j * chains, total, 0.0), axis=1, keepdims=True)
                for j in range(len(sums))
            ]

        return finish

    unsent = []
    zero = jnp.zeros((chains, 128), F32)

    for load in patterns + loads[:1]:
        load.wait()
    for load in loads[1:]:
        load.start()
    def round_step(b, _):
        v[b] = x[:, cols(b)].astype(jnp.bfloat16)
        return 0

    lax.fori_loop(0, blocks, round_step, 0, unroll=4)
    send_halo(0, lambda b: v[b])
    order, last, count = sort_tables(ipat[0, 1:2, :], ipat[0, 0:1, :], n_inner)
    tab[0:1, 0:n_inner] = order
    tab[1:2, 0:n_inner] = jnp.where(count > 0, last, n_inner)
    lane128 = lax.broadcasted_iota(I32, (1, 128), 1)
    brow = jnp.full((1, 128), 1 << 20, I32)
    for k in range(4):
        for e in range(halo):
            brow = jnp.where(lane128 == k * halo + e, bpat[0, k, 0, e], brow)
    order, last, count = sort_tables(brow, jnp.zeros((1, 128), I32), 128)
    tab[2:3, 0:128] = order
    tab[3:4, 0:128] = jnp.where(count > 0, last, n_bnd)
    tables = pltpu.make_async_copy(tab, tab_s, local_sem.at[7])
    tables.start()
    run[n_inner] = jnp.zeros((chains, 128), F32)
    runb[n_bnd] = jnp.zeros((chains, 128), F32)

    tables.wait()
    for load in loads[1:]:
        load.wait()
    apply_parts(0)

    def first_step(b, _):
        value = rhs[:, cols(b)] - mapped_of(b)
        r[b] = value
        v[b] = value.astype(jnp.bfloat16)
        return 0

    lax.fori_loop(0, blocks, first_step, 0, unroll=4)
    send_halo(1, lambda b: v[b])
    apply_parts(1)

    def dots_step(b, sums):
        value = mapped_of(b)
        res = r[b]
        wb[b] = value
        return sums[0] + res * res, sums[1] + res * value, sums[2] + value * value

    sums = lax.fori_loop(0, blocks, dots_step, (zero, zero, zero), unroll=4)
    norm, cross, square = all_sum(0, sums)()
    step = norm / cross
    norm_next = norm - 2.0 * step * cross + step * step * square
    ratio = norm_next / norm
    step_b = jnp.broadcast_to(step, (chains, 128))
    ratio_b = jnp.broadcast_to(ratio, (chains, 128))

    def updated(b):
        old = r[b]
        value = old - step_b * wb[b]
        return value, value + ratio_b * old

    send_halo(2, lambda b: updated(b)[1])

    def update_step(b, rr):
        value, along = updated(b)
        rhs[:, cols(b)] = value
        d[:, cols(b)] = along
        v[b] = along.astype(jnp.bfloat16)
        return rr + value * value

    rr = lax.fori_loop(0, blocks, update_step, zero, unroll=4)
    stores = [
        pltpu.make_async_copy(rhs, r_hbm, local_sem.at[9]),
        pltpu.make_async_copy(d, d_hbm, local_sem.at[10]),
    ]
    for store in stores:
        store.start()
    apply_parts(2)

    def last_dot_step(b, total):
        value = mapped_of(b)
        w[:, cols(b)] = value
        return total + d[:, cols(b)] * value

    dw = lax.fori_loop(0, blocks, last_dot_step, zero, unroll=4)
    stores.append(pltpu.make_async_copy(w, w_hbm, local_sem.at[13]))
    stores[-1].start()
    finish = all_sum(1, (rr, dw))

    def x_step(b, _):
        x[:, cols(b)] = x[:, cols(b)] + step_b * r[b]
        return 0

    lax.fori_loop(0, blocks, x_step, 0, unroll=4)
    stores.append(pltpu.make_async_copy(x, x_hbm, local_sem.at[8]))
    stores[-1].start()
    norm, curve = finish()
    step_c = jnp.broadcast_to(norm / curve, (chains, 128))

    alpha[...] = step_c
    stores.append(pltpu.make_async_copy(alpha, alpha_hbm, local_sem.at[14]))
    stores[-1].start()
    for turn in range(3):
        for k in range(4):
            box_copy(turn, k).wait_send()
    for wait in unsent:
        wait()
    for store in stores:
        store.wait()


def per_device(nr, nd, inner_blocks, inner_pattern, boundary_blocks, boundary_pattern, send_list, right_side, initial):
    n_inner, blk = inner_blocks.shape[1], inner_blocks.shape[2]
    halo = send_list.shape[2]
    chains, nodes = right_side.shape
    blocks = nodes // blk
    anywhere = pl.BlockSpec(memory_space=pl.ANY)
    vector = pltpu.VMEM((chains, nodes), F32)
    x, r, d, w, step = pl.pallas_call(
        functools.partial(kernel, nr, nd),
        out_shape=(jax.ShapeDtypeStruct((chains, nodes), F32),) * 4
        + (jax.ShapeDtypeStruct((chains, 128), F32),),
        in_specs=[pl.BlockSpec(memory_space=pltpu.HBM)] * 7,
        out_specs=(anywhere,) * 5,
        scratch_shapes=[
            pltpu.VMEM(inner_pattern.shape, I32),
            pltpu.SMEM(boundary_pattern.shape, I32),
            pltpu.SMEM(send_list.shape, I32),
            pltpu.VMEM((n_inner, blk, blk), jnp.bfloat16),
            pltpu.VMEM((4, halo, blk, blk), jnp.bfloat16),
            pltpu.VMEM((blocks, chains, blk), F32),
            pltpu.VMEM((blocks, chains, blk), F32),
            vector,
            vector,
            vector,
            vector,
            pltpu.VMEM((chains, 128), F32),
            pltpu.VMEM((blocks, chains, blk), jnp.bfloat16),
            pltpu.VMEM((n_inner + 1, chains, blk), F32),
            pltpu.VMEM((4 * halo + 1, chains, blk), F32),
            pltpu.VMEM((4 * halo, chains, blk), F32),
            pltpu.VMEM((3, 4, halo, chains, blk), jnp.bfloat16),
            pltpu.VMEM((8, 256), I32),
            pltpu.SMEM((8, 256), I32),
            pltpu.VMEM((ITERS, nr * nd, 1, 128), F32),
            pltpu.SemaphoreType.DMA((15,)),
            pltpu.SemaphoreType.DMA((3, 4)),
            pltpu.SemaphoreType.DMA((3, 4)),
            pltpu.SemaphoreType.DMA((ITERS, 2, nr * nd)),
        ]
        + [pltpu.VMEM((halo, chains, blk), jnp.bfloat16)] * 12,
        compiler_params=pltpu.CompilerParams(
            collective_id=0, has_side_effects=True, vmem_limit_bytes=48 * 1024 * 1024
        ),
    )(inner_blocks, inner_pattern, boundary_blocks, boundary_pattern, send_list, right_side, initial)
    step = step[:, :1]
    return x + step * d, r - step * w


def solution(mesh):
    spread = ("groups", "region", "dev")
    return jax.shard_map(
        functools.partial(per_device, mesh.shape["region"], mesh.shape["dev"]),
        mesh=mesh,
        in_specs=(
            P(spread, None, None, None),
            P(spread, None, None),
            P(spread, None, None, None, None),
            P(spread, None, None, None),
            P(spread, None, None),
            P(None, spread),
            P(None, spread),
        ),
        out_specs=(P(None, spread), P(None, spread)),
        check_vma=False,
    )
```

```python
import functools

import jax
import jax.numpy as jnp
from jax import lax
from jax.experimental import pallas as pl
from jax.experimental.pallas import tpu as pltpu
from jax.sharding import PartitionSpec as P

MESH = pl.DeviceIdType.MESH
ITERS = 2
F32 = jnp.float32
I32 = jnp.int32


def to_sublanes(values, square):
    return jnp.sum(jnp.where(square, values, 0), axis=1, keepdims=True)


def sort_tables(row_lane, col_lane, length):
    lane = lax.broadcasted_iota(I32, (length, length), 1)
    sub = lax.broadcasted_iota(I32, (length, length), 0)
    eye = lane == sub
    key_lane = row_lane * 256 + lax.broadcasted_iota(I32, (1, length), 1)
    key_sub = to_sublanes(key_lane, eye)
    row_sub = to_sublanes(row_lane, eye)
    col_sub = to_sublanes(col_lane, eye)
    rank = jnp.sum(jnp.where(key_lane < key_sub, 1, 0), axis=1, keepdims=True)
    less = jnp.sum(jnp.where(row_lane < row_sub, 1, 0), axis=1, keepdims=True)
    keep = jnp.where(rank == less, 0, 1)
    packed = (key_sub - row_sub * 256) + keep * 256 + col_sub * 512
    order = jnp.sum(jnp.where(rank == lane, packed, 0), axis=0, keepdims=True)
    upto = jnp.sum(jnp.where(row_sub <= lane, 1, 0), axis=0, keepdims=True)
    count = jnp.sum(jnp.where(row_sub == lane, 1, 0), axis=0, keepdims=True)
    return order, upto - 1, count


def kernel(
    nr, nd, inner_hbm, ipat_hbm, bnd_hbm, bpat_hbm, send_hbm, rhs_hbm, init_hbm, x_hbm, r_hbm, d_hbm, w_hbm, alpha_hbm,
    ipat, bpat, send_list, q, qb, r, wb, x, rhs, w, d, alpha, v, run, runb, prodb, out_box, tab, tab_s, slots,
    local_sem, out_sem, in_sem, sems, *in_box,
):
    n_inner = q.shape[0]
    halo = out_box.shape[2]
    n_bnd = 4 * halo
    blocks = v.shape[0]
    chains = v.shape[1]
    region, dev = lax.axis_index("region"), lax.axis_index("dev")
    n_all = nr * nd
    me = region * nd + dev

    def each_peer(action):
        if n_all <= 16:
            for t in range(1, n_all):
                action(t)
        else:
            lax.fori_loop(1, n_all, lambda t, _: (action(t), 0)[1], 0)

    chunk = n_inner // 4
    loads = [pltpu.make_async_copy(init_hbm, x, local_sem.at[0])]
    for i in range(4):
        part_of = pl.ds(i * chunk, chunk)
        loads.append(pltpu.make_async_copy(inner_hbm.at[0, part_of], q.at[part_of], local_sem.at[1 + i]))
    loads.append(pltpu.make_async_copy(bnd_hbm.at[0], qb, local_sem.at[5]))
    loads.append(pltpu.make_async_copy(rhs_hbm, rhs, local_sem.at[6]))
    patterns = [
        pltpu.make_async_copy(ipat_hbm, ipat, local_sem.at[10]),
        pltpu.make_async_copy(bpat_hbm, bpat, local_sem.at[11]),
        pltpu.make_async_copy(send_hbm, send_list, local_sem.at[12]),
    ]
    for load in patterns + loads[:1]:
        load.start()

    barrier = pltpu.get_barrier_semaphore()
    def greet(t):
        peer = lax.rem(me + t, n_all)
        pl.semaphore_signal(
            barrier, inc=1, device_id={"region": peer // nd, "dev": lax.rem(peer, nd)}, device_id_type=MESH
        )

    each_peer(greet)

    targets = (
        {"dev": lax.rem(dev + nd - 1, nd)},
        {"dev": lax.rem(dev + 1, nd)},
        {"region": lax.rem(region + nr - 1, nr)},
        {"region": lax.rem(region + 1, nr)},
    )
    arrives_at = (1, 0, 3, 2)

    def cols(b):
        return pl.ds(pl.multiple_of(b * 128, 128), 128)

    def box_copy(turn, k):
        return pltpu.make_async_remote_copy(
            src_ref=out_box.at[turn, k],
            dst_ref=in_box[turn * 4 + arrives_at[k]],
            send_sem=out_sem.at[turn, k],
            recv_sem=in_sem.at[turn, arrives_at[k]],
            device_id=targets[k],
            device_id_type=MESH,
        )

    def send_halo(turn, block_of):
        for k in (0, 1, 2, 3):
            for e in range(halo):
                out_box[turn, k, e] = block_of(send_list[0, k, e]).astype(jnp.bfloat16)
            if turn == 0 and k == 0:
                pl.semaphore_wait(barrier, n_all - 1)
            box_copy(turn, k).start()

    def apply_parts(turn):
        def inner_step(s, acc):
            word = tab_s[0, s]
            entry, keep, col = word & 255, (word >> 8) & 1, word >> 9
            product = jnp.dot(v[col], q[entry], preferred_element_type=F32)
            acc = jnp.where(jnp.full((chains, 128), keep) != 0, acc, 0.0) + product
            run[s] = acc
            return acc

        lax.fori_loop(0, n_inner, inner_step, jnp.zeros((chains, 128), F32), unroll=32)
        for k in (2, 3, 0, 1):
            box_copy(turn, arrives_at[k]).wait_recv()

            def far_step(e, _):
                prodb[k * halo + e] = lax.dot_general(
                    in_box[turn * 4 + k][bpat[0, k, 1, e]],
                    qb[k, e],
                    (((1,), (1,)), ((), ())),
                    preferred_element_type=F32,
                )
                return 0

            lax.fori_loop(0, halo, far_step, 0, unroll=True)

        def gather_step(s, acc):
            word = tab_s[2, s]
            entry, keep = word & 255, (word >> 8) & 1
            acc = jnp.where(jnp.full((chains, 128), keep) != 0, acc, 0.0) + prodb[entry]
            runb[s] = acc
            return acc

        lax.fori_loop(0, n_bnd, gather_step, jnp.zeros((chains, 128), F32), unroll=8)

    def mapped_of(b):
        return run[tab_s[1, b]] + runb[tab_s[3, b]]

    chain = lax.broadcasted_iota(I32, (chains, 128), 0)
    lane = lax.broadcasted_iota(I32, (chains, 128), 1)

    def all_sum(turn, sums):
        packed = jnp.zeros((chains, 128), F32)
        for j, value in enumerate(sums):
            packed = packed + jnp.where(
                lane == chain + j * chains, jnp.sum(value, axis=1, keepdims=True), 0.0
            )
        row = jnp.sum(packed, axis=0, keepdims=True)
        slots[turn, me] = row

        def copy(t, at):
            peer = lax.rem(me + n_all - t, n_all)
            slot = me if at else peer
            return pltpu.make_async_remote_copy(
                src_ref=slots.at[turn, me],
                dst_ref=slots.at[turn, slot],
                send_sem=sems.at[turn, 0, peer],
                recv_sem=sems.at[turn, 1, slot],
                device_id={"region": peer // nd, "dev": lax.rem(peer, nd)},
                device_id_type=MESH,
            )

        each_peer(lambda t: copy(t, True).start())
        unsent.append(lambda: each_peer(lambda t: copy(t, True).wait_send()))

        def finish():
            each_peer(lambda t: copy(t, False).wait_recv())
            total = jnp.sum(slots[turn].reshape(n_all, 128), axis=0, keepdims=True)
            return [
                jnp.sum(jnp.where(lane == chain + j * chains, total, 0.0), axis=1, keepdims=True)
                for j in range(len(sums))
            ]

        return finish

    unsent = []
    zero = jnp.zeros((chains, 128), F32)

    for load in patterns + loads[:1]:
        load.wait()
    for load in loads[1:]:
        load.start()
    def round_step(b, _):
        v[b] = x[:, cols(b)].astype(jnp.bfloat16)
        return 0

    lax.fori_loop(0, blocks, round_step, 0, unroll=8)
    send_halo(0, lambda b: v[b])
    order, last, count = sort_tables(ipat[0, 1:2, :], ipat[0, 0:1, :], n_inner)
    tab[0:1, 0:n_inner] = order
    tab[1:2, 0:n_inner] = jnp.where(count > 0, last, n_inner)
    lane128 = lax.broadcasted_iota(I32, (1, 128), 1)
    brow = jnp.full((1, 128), 1 << 20, I32)
    for k in range(4):
        for e in range(halo):
            brow = jnp.where(lane128 == k * halo + e, bpat[0, k, 0, e], brow)
    order, last, count = sort_tables(brow, jnp.zeros((1, 128), I32), 128)
    tab[2:3, 0:128] = order
    tab[3:4, 0:128] = jnp.where(count > 0, last, n_bnd)
    tables = pltpu.make_async_copy(tab, tab_s, local_sem.at[7])
    tables.start()
    run[n_inner] = jnp.zeros((chains, 128), F32)
    runb[n_bnd] = jnp.zeros((chains, 128), F32)

    tables.wait()
    for load in loads[1:]:
        load.wait()
    apply_parts(0)

    def first_step(b, _):
        value = rhs[:, cols(b)] - mapped_of(b)
        r[b] = value
        v[b] = value.astype(jnp.bfloat16)
        return 0

    lax.fori_loop(0, blocks, first_step, 0, unroll=8)
    send_halo(1, lambda b: v[b])
    apply_parts(1)

    def dots_step(b, sums):
        value = mapped_of(b)
        res = r[b]
        wb[b] = value
        return sums[0] + res * res, sums[1] + res * value, sums[2] + value * value

    sums = lax.fori_loop(0, blocks, dots_step, (zero, zero, zero), unroll=8)
    norm, cross, square = all_sum(0, sums)()
    step = norm / cross
    norm_next = norm - 2.0 * step * cross + step * step * square
    ratio = norm_next / norm
    step_b = jnp.broadcast_to(step, (chains, 128))
    ratio_b = jnp.broadcast_to(ratio, (chains, 128))

    def updated(b):
        old = r[b]
        value = old - step_b * wb[b]
        return value, value + ratio_b * old

    send_halo(2, lambda b: updated(b)[1])

    def update_step(b, rr):
        value, along = updated(b)
        rhs[:, cols(b)] = value
        d[:, cols(b)] = along
        v[b] = along.astype(jnp.bfloat16)
        return rr + value * value

    rr = lax.fori_loop(0, blocks, update_step, zero, unroll=8)
    stores = [
        pltpu.make_async_copy(rhs, r_hbm, local_sem.at[9]),
        pltpu.make_async_copy(d, d_hbm, local_sem.at[10]),
    ]
    for store in stores:
        store.start()
    apply_parts(2)

    def last_dot_step(b, total):
        value = mapped_of(b)
        w[:, cols(b)] = value
        return total + d[:, cols(b)] * value

    dw = lax.fori_loop(0, blocks, last_dot_step, zero, unroll=8)
    stores.append(pltpu.make_async_copy(w, w_hbm, local_sem.at[13]))
    stores[-1].start()
    finish = all_sum(1, (rr, dw))

    def x_step(b, _):
        x[:, cols(b)] = x[:, cols(b)] + step_b * r[b]
        return 0

    lax.fori_loop(0, blocks, x_step, 0, unroll=8)
    stores.append(pltpu.make_async_copy(x, x_hbm, local_sem.at[8]))
    stores[-1].start()
    norm, curve = finish()
    step_c = jnp.broadcast_to(norm / curve, (chains, 128))

    alpha[...] = step_c
    stores.append(pltpu.make_async_copy(alpha, alpha_hbm, local_sem.at[14]))
    stores[-1].start()
    for turn in range(3):
        for k in range(4):
            box_copy(turn, k).wait_send()
    for wait in unsent:
        wait()
    for store in stores:
        store.wait()


def per_device(nr, nd, inner_blocks, inner_pattern, boundary_blocks, boundary_pattern, send_list, right_side, initial):
    n_inner, blk = inner_blocks.shape[1], inner_blocks.shape[2]
    halo = send_list.shape[2]
    chains, nodes = right_side.shape
    blocks = nodes // blk
    anywhere = pl.BlockSpec(memory_space=pl.ANY)
    vector = pltpu.VMEM((chains, nodes), F32)
    x, r, d, w, step = pl.pallas_call(
        functools.partial(kernel, nr, nd),
        out_shape=(jax.ShapeDtypeStruct((chains, nodes), F32),) * 4
        + (jax.ShapeDtypeStruct((chains, 128), F32),),
        in_specs=[pl.BlockSpec(memory_space=pltpu.HBM)] * 7,
        out_specs=(anywhere,) * 5,
        scratch_shapes=[
            pltpu.VMEM(inner_pattern.shape, I32),
            pltpu.SMEM(boundary_pattern.shape, I32),
            pltpu.SMEM(send_list.shape, I32),
            pltpu.VMEM((n_inner, blk, blk), jnp.bfloat16),
            pltpu.VMEM((4, halo, blk, blk), jnp.bfloat16),
            pltpu.VMEM((blocks, chains, blk), F32),
            pltpu.VMEM((blocks, chains, blk), F32),
            vector,
            vector,
            vector,
            vector,
            pltpu.VMEM((chains, 128), F32),
            pltpu.VMEM((blocks, chains, blk), jnp.bfloat16),
            pltpu.VMEM((n_inner + 1, chains, blk), F32),
            pltpu.VMEM((4 * halo + 1, chains, blk), F32),
            pltpu.VMEM((4 * halo, chains, blk), F32),
            pltpu.VMEM((3, 4, halo, chains, blk), jnp.bfloat16),
            pltpu.VMEM((8, 256), I32),
            pltpu.SMEM((8, 256), I32),
            pltpu.VMEM((ITERS, nr * nd, 1, 128), F32),
            pltpu.SemaphoreType.DMA((15,)),
            pltpu.SemaphoreType.DMA((3, 4)),
            pltpu.SemaphoreType.DMA((3, 4)),
            pltpu.SemaphoreType.DMA((ITERS, 2, nr * nd)),
        ]
        + [pltpu.VMEM((halo, chains, blk), jnp.bfloat16)] * 12,
        compiler_params=pltpu.CompilerParams(
            collective_id=0, has_side_effects=True, vmem_limit_bytes=49 * 1024 * 1024
        ),
    )(inner_blocks, inner_pattern, boundary_blocks, boundary_pattern, send_list, right_side, initial)
    step = step[:, :1]
    return x + step * d, r - step * w


def solution(mesh):
    spread = ("groups", "region", "dev")
    return jax.shard_map(
        functools.partial(per_device, mesh.shape["region"], mesh.shape["dev"]),
        mesh=mesh,
        in_specs=(
            P(spread, None, None, None),
            P(spread, None, None),
            P(spread, None, None, None, None),
            P(spread, None, None, None),
            P(spread, None, None),
            P(None, spread),
            P(None, spread),
        ),
        out_specs=(P(None, spread), P(None, spread)),
        check_vma=False,
    )
```
